256 devices in a mesh: sec: 4 (over x), en: 64 (over y, z, core).
Axes of the slice: x: 4, y: 4, z: 8, core: 2. Of those that a mesh axis runs over, the one named last changes fastest.
Arguments:
- inverse_blocks: float32 [4, 256, 2, 256, 256], P('sec', 'en')
- coupling: float32 [4, 256, 256], P('sec'), may hold values from -0.375 to 0.375
- boundary: float32 [256, 2, 256, 256], P('en')
- band_offsets: int32 [6], replicated, may hold values from -2 to 2, as said below
- band_weights: float32 [4, 6], P('sec'), may hold values from 0.1 to 1
Outputs:
- green_blocks: float32 [4, 256, 2, 256, 256], P('sec', 'en')
- self_energy: float32 [4, 256, 2, 256, 256], P('sec', 'en')
The draws below stay inside these ranges and needn't reach their ends.
Inputs may be any that keep to these rules, and one draw needn't show every extreme that they name: `band_offsets`: every offset lies within -2 to 2, and both ends occur in every draw.
All inputs are finite; a program needn't handle non-finite values.
Results may differ from the reference program's by a relative error of at most 0.00011.
Values sent between devices are 32-bit elements; how exact they have to be, the bound alone decides.
No kernel may reach another device: no remote copies, remote signals or barrier semaphores. Data moves between devices by JAX's collectives and lax.ppermute only.
A program may use at most 128 MiB of HBM per device.

```python
import math
import jax
import jax.numpy as jnp
from jax import lax

ORB = 256
BANDS = 6
MAXOFF = 2
SLICES = 4
ENERGIES = 256


def block_draw(key, lead_shape):
    key_off, key_real, key_imag = jax.random.split(key, 3)
    full_shape = tuple(lead_shape) + (2, ORB, ORB)
    spread = 0.25 / ORB ** 0.5
    off_part = jax.random.normal(key_off, full_shape, jnp.float32) * spread
    diag_real = jax.random.uniform(key_real, tuple(lead_shape) + (ORB,), jnp.float32, 0.5, 0.9)
    diag_imag = jax.random.uniform(key_imag, tuple(lead_shape) + (ORB,), jnp.float32, -0.6, -0.2)
    eye_mat = jnp.eye(ORB, dtype=jnp.float32)
    diag_part = jnp.stack([eye_mat * diag_real[..., :, None], eye_mat * diag_imag[..., :, None]], axis=-3)
    return off_part + diag_part


def draw_inverse_blocks(key, part):
    return block_draw(jax.random.fold_in(key, 11), (SLICES, ENERGIES))


def draw_boundary(key, part):
    return block_draw(jax.random.fold_in(key, 23), (ENERGIES,))


def draw_band_offsets(key, part):
    key_vals, key_perm = jax.random.split(jax.random.fold_in(key, 37))
    others = jax.random.randint(key_vals, (BANDS - 2,), 0 - MAXOFF, MAXOFF + 1, jnp.int32)
    ends = jnp.array([MAXOFF, 0 - MAXOFF], jnp.int32)
    return jax.random.permutation(key_perm, jnp.concatenate([ends, others]))


def levels(stream_key, extent, cuts, low, top_value):
    def one(position, blocks):
        steps = jax.random.uniform(jax.random.fold_in(jax.random.fold_in(stream_key, 6), position), (blocks,), jnp.float32, low / len(cuts), top_value / len(cuts))
        return jnp.repeat(jnp.exp(steps), extent[position] // blocks).reshape((-1,) + (1,) * (len(extent) - position - 1))

    gain = one(*cuts[0])
    for cut in cuts[1:]:
        gain = gain * one(*cut)
    return gain


def scatter_about(own_key, shape, scale, bound, cuts=(), kind=jnp.bfloat16):
    result = jax.random.normal(own_key, shape, jnp.float32) * scale
    if len(cuts) > 0:
        result = levels(own_key, shape, cuts, -0.22, 0.18) * result
    return jnp.clip(result, min=-bound, max=bound).astype(kind)


def setup_inputs(seed: int = 0) -> dict:
    key_of = jax.random.split(jax.random.key(seed), 6)
    inverse_blocks = draw_inverse_blocks(jax.random.fold_in(key_of[5], 71), 0)
    coupling = scatter_about(key_of[1], (SLICES, ORB, ORB), ORB ** -0.5, 0.375, ((0, 4),), jnp.float32)
    boundary = draw_boundary(jax.random.fold_in(key_of[5], 71), 0)
    band_offsets = draw_band_offsets(jax.random.fold_in(key_of[5], 71), 0)
    band_weights = jnp.clip(jnp.exp(math.log(1.0) - 2.3025851 * jax.random.uniform(key_of[4], (SLICES, BANDS), jnp.float32) ** levels(key_of[4], (SLICES, BANDS), ((0, 4),), -0.2, 0.2)), 0.1, 1.0)
    return {"inverse_blocks": inverse_blocks, "coupling": coupling, "boundary": boundary, "band_offsets": band_offsets, "band_weights": band_weights}


def batch_product(left, right):
    return jnp.einsum("eij,ejk->eik", left, right, precision=lax.Precision.HIGHEST)


def complex_mul(left, right):
    real_part = batch_product(left[:, 0], right[:, 0]) - batch_product(left[:, 1], right[:, 1])
    imag_part = batch_product(left[:, 0], right[:, 1]) + batch_product(left[:, 1], right[:, 0])
    return jnp.stack([real_part, imag_part], axis=1)


def real_right(left, matrix):
    return jnp.einsum("exij,jk->exik", left, matrix, precision=lax.Precision.HIGHEST)


def conv_matrix(weights_row, offsets, rows_n, cols_n, shift):
    row_pos = jnp.arange(rows_n, dtype=jnp.int32)
    col_pos = jnp.arange(cols_n, dtype=jnp.int32)
    hits = (col_pos[None, None, :] == row_pos[None, :, None] + shift + offsets[:, None, None]).astype(jnp.float32)
    return jnp.sum(weights_row[:, None, None] * hits, axis=0)


def reference(inverse_blocks, coupling, boundary, band_offsets, band_weights):
    current = boundary
    greens = []
    for slice_no in range(SLICES):
        transfer = real_right(inverse_blocks[slice_no], coupling[slice_no])
        current = complex_mul(complex_mul(transfer, current), jnp.swapaxes(transfer, -1, -2)) + inverse_blocks[slice_no]
        greens.append(current)
    green_blocks = jnp.stack(greens, axis=0)
    sigmas = []
    for slice_no in range(SLICES):
        weights_mat = conv_matrix(band_weights[slice_no], band_offsets, ENERGIES, ENERGIES, 0)
        sigmas.append(jnp.einsum("ef,fxij->exij", weights_mat, green_blocks[slice_no], precision=lax.Precision.HIGHEST))
    self_energy = jnp.stack(sigmas, axis=0)
    return green_blocks, self_energy
```

```python
import jax
import jax.numpy as jnp
from jax import lax
from jax.experimental import pallas as pl
from jax.experimental.pallas import tpu as pltpu
from jax.sharding import PartitionSpec as P

F32 = jnp.float32
BF16 = jnp.bfloat16
NN = (((1,), (0,)), ((), ()))
NT = (((1,), (1,)), ((), ()))


def split(value):
    high = value.astype(BF16)
    return high, (value - high.astype(F32)).astype(BF16)


def dot3(left, right, dims):
    def one(a, b):
        return lax.dot_general(a, b, dims, preferred_element_type=F32)

    return one(left[0], right[0]) + (one(left[0], right[1]) + one(left[1], right[0]))


def complex_blocks(product):
    orb = product.shape[0] // 2
    real = product[:orb, :orb] - product[orb:, orb:]
    imag = product[:orb, orb:] + product[orb:, :orb]
    return real, imag


def chain_kernel(parts, scalars, own, *refs):
    arrived = refs[: parts - 1]
    coupling, boundary = refs[parts - 1 : parts + 1]
    outs = refs[parts + 1 : 2 * parts + 1]
    inverse, previous = refs[2 * parts + 1 :]
    me = scalars[0]
    orb = coupling.shape[-1]
    previous[0] = boundary[0, 0]
    previous[1] = boundary[0, 1]
    for stage in range(parts):
        slot = lax.rem(me - stage + parts, parts)
        for number in range(parts):

            @pl.when(slot == number)
            def _():
                source = own if number == 0 else arrived[number - 1]
                inverse[0] = source[0, 0]
                inverse[1] = source[0, 1]

        own_inverse = inverse[...]
        transfer = dot3(split(own_inverse.reshape(2 * orb, orb)), split(coupling[stage]), NN)
        transfer = split(transfer)
        before = split(jnp.concatenate([previous[0], previous[1]], axis=1))
        half = jnp.concatenate(complex_blocks(dot3(transfer, before, NN)), axis=0)
        real, imag = complex_blocks(dot3(split(half), transfer, NT))
        real = real + own_inverse[0]
        imag = imag + own_inverse[1]
        if stage < parts - 1:
            previous[0] = real
            previous[1] = imag
        target = lax.rem(stage - me + parts, parts)
        for number in range(parts):

            @pl.when(target == number)
            def _():
                outs[number][0, 0] = real
                outs[number][0, 1] = imag


def run_chain(me, inverse_blocks, arrived, couplings, boundary):
    parts, orb, _ = couplings.shape
    block = (1, 2, orb, orb)

    def mine(step, scalars):
        return (scalars[0], 0, 0, 0)

    def whole(step, scalars):
        return (0, 0, 0, 0)

    picked = pl.BlockSpec(block, mine)
    plain = pl.BlockSpec(block, whole)
    return pl.pallas_call(
        lambda *refs: chain_kernel(parts, *refs),
        out_shape=[jax.ShapeDtypeStruct(block, F32)] * parts,
        grid_spec=pltpu.PrefetchScalarGridSpec(
            num_scalar_prefetch=1,
            grid=(1,),
            in_specs=[picked]
            + [plain] * (parts - 1)
            + [pl.BlockSpec((parts, orb, orb), lambda step, scalars: (0, 0, 0)), picked],
            out_specs=[plain] * parts,
            scratch_shapes=[pltpu.VMEM((2, orb, orb), F32)] * 2,
        ),
        compiler_params=pltpu.CompilerParams(vmem_limit_bytes=48 * 1024 * 1024),
        cost_estimate=pl.CostEstimate(
            flops=parts * 60 * orb**3, bytes_accessed=parts * 20 * orb * orb, transcendentals=0
        ),
        name="chain",
    )(me[None], inverse_blocks, *arrived, couplings, boundary)


def band_kernel(count, scalars, *refs):
    weights = refs[0]
    slots = refs[1 : 2 * count + 1]
    green, energy = refs[2 * count + 1 :]
    me = scalars[0]
    values = [slot[0] for slot in slots]
    for number in range(count):
        green[lax.rem(me - number + count, count)] = values[number]
    for row in range(count):
        total = weights[row, 0] * values[0]
        for number in range(1, 2 * count):
            total = total + weights[row, number] * values[number]
        energy[row] = total


def run_band(me, weights, slots):
    count, (_, _, orb, _) = len(slots) // 2, slots[0].shape
    chunks = 4
    rows = orb // chunks
    part = pl.BlockSpec((1, 2, rows, orb), lambda step, scalars: (0, 0, step, 0))
    whole = pl.BlockSpec((count, 2, rows, orb), lambda step, scalars: (0, 0, step, 0))
    return pl.pallas_call(
        lambda *refs: band_kernel(count, *refs),
        out_shape=[jax.ShapeDtypeStruct((count, 2, orb, orb), F32)] * 2,
        grid_spec=pltpu.PrefetchScalarGridSpec(
            num_scalar_prefetch=1,
            grid=(chunks,),
            in_specs=[pl.BlockSpec(memory_space=pltpu.SMEM)] + [part] * (2 * count),
            out_specs=[whole] * 2,
        ),
        compiler_params=pltpu.CompilerParams(vmem_limit_bytes=48 * 1024 * 1024),
        name="band",
    )(me[None], weights, *slots)


def on_device(inverse_blocks, coupling, boundary, band_offsets, band_weights):
    parts, devices = lax.axis_size("sec"), lax.axis_size("en")
    own_inverse = inverse_blocks[0]
    count = own_inverse.shape[0]
    me = lax.axis_index("sec")
    both = ("sec", "en")

    orb = coupling.shape[-1]
    rows = orb // devices
    piece = lax.dynamic_slice(coupling[0], (lax.axis_index("en") * rows, 0), (rows, orb))
    couplings = lax.all_gather(piece, both, axis=0, tiled=True).reshape(parts, orb, orb)

    arrived = []
    for shift in range(1, parts):
        sent = lax.dynamic_slice_in_dim(own_inverse, lax.rem(me + shift, parts), 1, axis=0)
        ring = [(source, (source + shift) % parts) for source in range(parts)]
        arrived.append(lax.ppermute(sent, "sec", ring))
    produced = run_chain(me, own_inverse, arrived, couplings, boundary)

    slots = [produced[0]]
    for shift in range(1, parts):
        ring = [(source, (source + shift) % parts) for source in range(parts)]
        slots.append(lax.ppermute(produced[shift], "sec", ring))
    halos = []
    for shift in range(parts):
        pairs = []
        for sec in range(parts):
            step = 1 if (sec - shift) % parts >= count // 2 else -1
            for en in range(devices):
                if 0 <= en + step < devices:
                    pairs.append((sec * devices + en, sec * devices + en + step))
        halos.append(lax.ppermute(slots[shift], both, pairs))

    local = lax.rem(me - jnp.arange(parts, dtype=jnp.int32) + parts, parts)
    beyond = jnp.where(local >= count // 2, local - count, local + count)
    place = jnp.concatenate([local, beyond])
    away = place[None, :] - jnp.arange(count, dtype=jnp.int32)[:, None]
    hits = (band_offsets[:, None, None] == away[None]).astype(F32)
    weights = jnp.sum(band_weights[0][:, None, None] * hits, axis=0)
    green_blocks, self_energy = run_band(me, weights, slots + halos)
    return green_blocks[None], self_energy[None]


def solution(mesh):
    return jax.shard_map(
        on_device,
        mesh=mesh,
        in_specs=(
            P("sec", "en", None, None, None),
            P("sec", None, None),
            P("en", None, None, None),
            P(),
            P("sec", None),
        ),
        out_specs=(P("sec", "en", None, None, None), P("sec", "en", None, None, None)),
        check_vma=False,
    )
```

```python
import jax
import jax.numpy as jnp
from jax import lax
from jax.experimental import pallas as pl
from jax.experimental.pallas import tpu as pltpu
from jax.sharding import PartitionSpec as P

F32 = jnp.float32
BF16 = jnp.bfloat16
NN = (((1,), (0,)), ((), ()))
NT = (((1,), (1,)), ((), ()))
VMEM = pl.BlockSpec(memory_space=pltpu.VMEM)
SMEM = pl.BlockSpec(memory_space=pltpu.SMEM)
HBM = pl.BlockSpec(memory_space=pltpu.HBM)
PARAMS = pltpu.CompilerParams(vmem_limit_bytes=36 * 1024 * 1024)
SMALL = pltpu.CompilerParams(vmem_limit_bytes=8 * 1024 * 1024)
def split(value):
    high = value.astype(BF16)
    return high, (value - high.astype(F32)).astype(BF16)


def dot3(left, right, dims):
    def one(a, b):
        return lax.dot_general(a, b, dims, preferred_element_type=F32)

    return one(left[0], right[0]) + (one(left[0], right[1]) + one(left[1], right[0]))


def triple(real, imag):
    return split(real), split(imag), split(real + imag)


def gauss(left, right, dims):
    first, second, third = (dot3(a, b, dims) for a, b in zip(left, right))
    return first - second, third - first - second


def store_transfer(inverse, coupling, high, low, stage):
    orb = coupling.shape[-1]
    both = dot3(split(inverse.reshape(2 * orb, orb)), split(coupling), NN)
    for number, (upper, lower) in enumerate(triple(both[:orb], both[orb:])):
        high[stage, number] = upper
        low[stage, number] = lower


def pick_kernel(me, inverse_all, boundary_all, kept, start, sems):
    copies = [
        pltpu.make_async_copy(inverse_all.at[me[0]], kept, sems.at[0]),
        pltpu.make_async_copy(boundary_all.at[me[0]], start, sems.at[1]),
    ]
    for copy in copies:
        copy.start()
    for copy in copies:
        copy.wait()


def run_pick(me, inverse_blocks, boundary):
    block = jax.ShapeDtypeStruct(inverse_blocks.shape[1:], F32)
    return pl.pallas_call(
        pick_kernel,
        out_shape=[block] * 2,
        in_specs=[SMEM] + [HBM] * 2,
        out_specs=[VMEM] * 2,
        scratch_shapes=[pltpu.SemaphoreType.DMA((2,))],
        compiler_params=SMALL,
        name="pick",
    )(me, inverse_blocks, boundary)


def chain_kernel(batch, parts, me_ref, core_ref, quarter_ref, kept, start, own_coupling, *refs):
    arrived = refs[: parts - 1]
    quarters = refs[parts - 1 : 2 * parts - 1]
    outs = refs[2 * parts - 1 : 3 * parts - 1]
    high, low, inverse, previous, coupling = refs[3 * parts - 1 :]
    me = me_ref[0]
    orb = coupling.shape[-1]
    rows = orb // len(quarters)

    @pl.when(lax.rem(me // 2 + core_ref[0], 2) == batch)
    def _():
        coupling[0] = own_coupling[0]
        for number, source in enumerate(quarters):
            quarter = lax.bitwise_xor(quarter_ref[0], number)
            place = pl.ds(pl.multiple_of(quarter * rows, rows), rows)
            for shift in range(1, parts):
                coupling[shift, place, :] = source[shift - 1]
        for shift in range(parts):
            stage = lax.rem(me - shift + parts, parts)
            inverse[stage] = kept[...] if shift == 0 else arrived[shift - 1][0]
            store_transfer(inverse[stage], coupling[shift], high, low, stage)
        previous[...] = start[...]
        for stage in range(parts):
            transfer = [(high[stage, number], low[stage, number]) for number in range(3)]
            half = gauss(transfer, triple(previous[0], previous[1]), NN)
            real, imag = gauss(triple(*half), transfer, NT)
            real = real + inverse[stage, 0]
            imag = imag + inverse[stage, 1]
            if stage < parts - 1:
                previous[0] = real
                previous[1] = imag
            target = lax.rem(stage - me + parts, parts)
            for number in range(parts):

                @pl.when(target == number)
                def _():
                    outs[number][0, 0] = real
                    outs[number][0, 1] = imag


def run_chain(batch, me, core, quarter, kept, start, coupling, arrived, quarters):
    parts = len(arrived) + 1
    orb = start.shape[-1]
    return pl.pallas_call(
        lambda *refs: chain_kernel(batch, parts, *refs),
        out_shape=[jax.ShapeDtypeStruct((1, 2, orb, orb), F32)] * parts,
        in_specs=[SMEM] * 3 + [VMEM] * (3 + len(arrived) + len(quarters)),
        out_specs=[VMEM] * parts,
        scratch_shapes=[
            pltpu.VMEM((parts, 3, orb, orb), BF16),
            pltpu.VMEM((parts, 3, orb, orb), BF16),
            pltpu.VMEM((parts, 2, orb, orb), F32),
            pltpu.VMEM((2, orb, orb), F32),
            pltpu.VMEM((parts, orb, orb), F32),
        ],
        compiler_params=PARAMS,
        cost_estimate=pl.CostEstimate(
            flops=parts * 48 * orb**3,
            bytes_accessed=parts * 20 * orb * orb,
            transcendentals=0,
        ),
        name="chain",
    )(me, core, quarter, kept, start, coupling, *arrived, *quarters)


def pack_kernel(batch, parts, me_ref, core_ref, *refs):
    sources, packed = refs[:parts], refs[parts]
    side = lax.bitwise_xor(core_ref[0], batch)
    for number in range(parts // 2):
        energy = side * (parts // 2) + number
        shift = lax.rem(me_ref[0] - energy + parts, parts)
        for which in range(parts):

            @pl.when(shift == which)
            def _():
                packed[number] = sources[which][0]


def run_pack(batch, me, core, sources):
    parts = len(sources)
    return pl.pallas_call(
        lambda *refs: pack_kernel(batch, parts, *refs),
        out_shape=jax.ShapeDtypeStruct((parts // 2,) + sources[0].shape[1:], F32),
        in_specs=[SMEM] * 2 + [VMEM] * parts,
        out_specs=VMEM,
        compiler_params=SMALL,
        name="pack",
    )(me, core, *sources)


def mix(weights, row, columns, values):
    total = weights[row, columns[0]] * values[0]
    for column, value in zip(columns[1:], values[1:]):
        total = total + weights[row, column] * value
    return total


ROWS = 32


def own_kernel(count, core_ref, weights, far, near, green, partial, sems):
    pair = count // 2
    orb = partial.shape[-1]
    core = core_ref[0]
    copies = []
    for number, (packed, base) in enumerate(((far, core * pair), (near, (1 - core) * pair))):
        copies.append(pltpu.make_async_copy(packed, green.at[pl.ds(base, pair)], sems.at[number]))
        copies[-1].start()
    for half in range(2):

        @pl.loop(0, orb // ROWS)
        def _(step):
            place = pl.ds(pl.multiple_of(step * ROWS, ROWS), ROWS)
            values = [ref[other, half, place, :] for ref in (far, near) for other in range(pair)]
            for row in range(count):
                partial[row, half, place, :] = mix(weights, row, (0, 1, 4, 5), values)

    for copy in copies:
        copy.wait()


def run_own(core, weights, far, near):
    count = weights.shape[0]
    whole = jax.ShapeDtypeStruct((count,) + far.shape[1:], F32)
    return pl.pallas_call(
        lambda *refs: own_kernel(count, *refs),
        out_shape=[whole] * 2,
        in_specs=[SMEM, SMEM, VMEM, VMEM],
        out_specs=[HBM, VMEM],
        scratch_shapes=[pltpu.SemaphoreType.DMA((2,))],
        compiler_params=SMALL,
        name="band_own",
    )(core, weights, far, near)


def admit_kernel(value, kept):
    pass


def run_admit(value):
    return pl.pallas_call(
        admit_kernel,
        out_shape=jax.ShapeDtypeStruct(value.shape, F32),
        in_specs=[VMEM],
        out_specs=VMEM,
        input_output_aliases={0: 0},
        compiler_params=SMALL,
        cost_estimate=pl.CostEstimate(flops=3_000_000_000, bytes_accessed=0, transcendentals=0),
        name="admit",
    )(value)


def halo_kernel(count, core_ref, weights, partial, near, far, energy, done, sems):
    pair = count // 2
    orb = partial.shape[-1]
    copies = []
    for halo, side, columns in ((near, 1 - core_ref[0], (6, 7)), (far, core_ref[0], (2, 3))):
        for number in range(pair):
            row = side * pair + number
            for half in range(2):

                @pl.loop(0, orb // ROWS)
                def _(step):
                    place = pl.ds(pl.multiple_of(step * ROWS, ROWS), ROWS)
                    values = [halo[other, half, place, :] for other in range(pair)]
                    done[row, half, place, :] = partial[row, half, place, :] + mix(
                        weights, row, columns, values
                    )

            copy = pltpu.make_async_copy(done.at[row], energy.at[row], sems.at[len(copies)])
            copy.start()
            copies.append(copy)
    for copy in copies:
        copy.wait()


def run_halo(core, weights, partial, near, far):
    count = weights.shape[0]
    return pl.pallas_call(
        lambda *refs: halo_kernel(count, *refs),
        out_shape=jax.ShapeDtypeStruct(partial.shape, F32),
        in_specs=[SMEM, SMEM, VMEM, VMEM, VMEM],
        out_specs=HBM,
        scratch_shapes=[pltpu.VMEM(partial.shape, F32), pltpu.SemaphoreType.DMA((count,))],
        compiler_params=SMALL,
        name="band_halo",
    )(core, weights, partial, near, far)


def on_device(inverse_blocks, coupling, boundary, band_offsets, band_weights):
    parts, devices = lax.axis_size("sec"), lax.axis_size("en")
    own_inverse = inverse_blocks[0]
    count = own_inverse.shape[0]
    pair = count // 2
    me, lane = lax.axis_index("sec"), lax.axis_index("en")
    orb = coupling.shape[-1]
    rows = orb // 4
    core = lax.rem(lane, 2)
    quarter = core + 2 * lax.rem(lane // 2 + lane // 16, 2)
    both = ("sec", "en")

    def ring(value, shift):
        pairs = [(source, (source + shift) % parts) for source in range(parts)]
        return lax.ppermute(value, "sec", pairs)

    def batch_pairs(batch, shift, to_runner):
        pairs = []
        for runner in range(parts):
            other = (runner - shift) % parts if to_runner else (runner + shift) % parts
            for en in range(devices):
                if (runner // 2 + en) % 2 == batch:
                    near, far = runner * devices + en, other * devices + en
                    pairs.append((far, near) if to_runner else (near, far))
        return pairs

    piece = lax.dynamic_slice(coupling, (0, quarter * rows, 0), (1, rows, orb))
    gathered = [ring(piece, shift) for shift in range(1, parts)]
    sent = [
        lax.dynamic_slice_in_dim(own_inverse, lax.rem(me + shift, parts), 1, axis=0)
        for shift in range(1, parts)
    ]
    def after(values, *waits):
        return list(lax.optimization_barrier((tuple(values), waits))[0])

    first = jnp.concatenate(gathered, axis=0)
    arrived = [
        [
            lax.ppermute(value, both, batch_pairs(batch, shift, True))
            for shift, value in enumerate(values, 1)
        ]
        for batch, values in enumerate((sent, sent))
    ]
    partners = (0, 1, 2, 17)
    quarters = [first] + [
        lax.ppermute(first, "en", [(source, source ^ partner) for source in range(devices)])
        for partner in partners[1:]
    ]
    kept, start = run_pick(me[None], own_inverse, boundary)

    packed = []
    for batch in range(2):
        produced = run_chain(
            batch, me[None], core[None], quarter[None], kept, start, coupling, arrived[batch], quarters
        )
        returned = [produced[0]] + [
            lax.ppermute(produced[shift], both, batch_pairs(batch, shift, False))
            for shift in range(1, parts)
        ]
        returned = after(returned, *packed)
        packed.append(run_pack(batch, me[None], core[None], returned))
    across = []
    for source in range(devices):
        target = source + 1 if source % 2 else source - 1
        if 0 <= target < devices:
            across.append((source, target))
    far_halo = lax.ppermute(packed[0], "en", across)
    near_halo = lax.ppermute(packed[1], "en", [(source, source ^ 1) for source in range(devices)])

    lower = jnp.arange(pair, dtype=jnp.int32)
    a_place, b_place = core * pair + lower, (1 - core) * pair + lower
    a_halo = jnp.where(core == 0, lower - pair, lower + count)
    b_halo = jnp.where(core == 0, lower + count, lower - pair)
    place = jnp.concatenate([a_place, a_halo, b_place, b_halo])
    away = place[None, :] - jnp.arange(count, dtype=jnp.int32)[:, None]
    hits = (band_offsets[:, None, None] == away[None]).astype(F32)
    weights = jnp.sum(band_weights[0][:, None, None] * hits, axis=0)
    core = core[None]
    green, partial = run_own(core, weights, *packed)
    energy = run_halo(core, weights, partial, near_halo, run_admit(far_halo))
    return green[None], energy[None]


def solution(mesh):
    return jax.shard_map(
        on_device,
        mesh=mesh,
        in_specs=(
            P("sec", "en", None, None, None),
            P("sec", None, None),
            P("en", None, None, None),
            P(),
            P("sec", None),
        ),
        out_specs=(P("sec", "en", None, None, None), P("sec", "en", None, None, None)),
        check_vma=False,
    )
```

```python
import jax
import jax.numpy as jnp
from jax import lax
from jax.experimental import pallas as pl
from jax.experimental.pallas import tpu as pltpu
from jax.sharding import PartitionSpec as P

F32 = jnp.float32
BF16 = jnp.bfloat16
NN = (((1,), (0,)), ((), ()))
NT = (((1,), (1,)), ((), ()))
VMEM = pl.BlockSpec(memory_space=pltpu.VMEM)
SMEM = pl.BlockSpec(memory_space=pltpu.SMEM)
HBM = pl.BlockSpec(memory_space=pltpu.HBM)
PARAMS = pltpu.CompilerParams(vmem_limit_bytes=36 * 1024 * 1024)
EARLY = (0, 1, 3)
ROWS = 32
LATE = 2
SMALL = pltpu.CompilerParams(vmem_limit_bytes=8 * 1024 * 1024)
def split(value):
    high = value.astype(BF16)
    return high, (value - high.astype(F32)).astype(BF16)


def dot3(left, right, dims):
    def one(a, b):
        return lax.dot_general(a, b, dims, preferred_element_type=F32)

    return one(left[0], right[0]) + (one(left[0], right[1]) + one(left[1], right[0]))


def triple(real, imag):
    return split(real), split(imag), split(real + imag)


def gauss(left, right, dims):
    first, second, third = (dot3(a, b, dims) for a, b in zip(left, right))
    return first - second, third - first - second


def store_transfer(inverse, coupling, high, low, stage):
    orb = coupling.shape[-1]
    both = dot3(split(inverse.reshape(2 * orb, orb)), split(coupling), NN)
    for number, (upper, lower) in enumerate(triple(both[:orb], both[orb:])):
        high[stage, number] = upper
        low[stage, number] = lower


def pick_kernel(me, inverse_all, boundary_all, kept, start, sems):
    copies = [
        pltpu.make_async_copy(inverse_all.at[me[0]], kept, sems.at[0]),
        pltpu.make_async_copy(boundary_all.at[me[0]], start, sems.at[1]),
    ]
    for copy in copies:
        copy.start()
    for copy in copies:
        copy.wait()


def run_pick(me, inverse_blocks, boundary):
    block = jax.ShapeDtypeStruct(inverse_blocks.shape[1:], F32)
    return pl.pallas_call(
        pick_kernel,
        out_shape=[block] * 2,
        in_specs=[SMEM] + [HBM] * 2,
        out_specs=[VMEM] * 2,
        scratch_shapes=[pltpu.SemaphoreType.DMA((2,))],
        compiler_params=SMALL,
        name="pick",
    )(me, inverse_blocks, boundary)


def chain_kernel(parts, me_ref, quarter_ref, kept, start, own_coupling, *refs):
    arrived = refs[: parts - 1]
    quarters = refs[parts - 1 : 2 * parts - 1]
    outs = refs[2 * parts - 1 : 3 * parts]
    high, low, inverse, previous, coupling = refs[3 * parts :]
    me = me_ref[0]
    orb = coupling.shape[-1]
    rows = orb // len(quarters)

    coupling[0] = own_coupling[0]
    for number, source in enumerate(quarters):
        quarter = lax.bitwise_xor(quarter_ref[0], number)
        place = pl.ds(pl.multiple_of(quarter * rows, rows), rows)
        for shift in range(1, parts):
            coupling[shift, place, :] = source[shift - 1]
    for shift in range(parts):
        stage = lax.rem(me - shift + parts, parts)
        inverse[stage] = kept[...] if shift == 0 else arrived[shift - 1][0]
        store_transfer(inverse[stage], coupling[shift], high, low, stage)
    previous[...] = start[...]
    for stage in range(parts):
        transfer = [(high[stage, number], low[stage, number]) for number in range(3)]
        half = gauss(transfer, triple(previous[0], previous[1]), NN)
        real, imag = gauss(triple(*half), transfer, NT)
        real = real + inverse[stage, 0]
        imag = imag + inverse[stage, 1]
        if stage < parts - 1:
            previous[0] = real
            previous[1] = imag
        target = lax.rem(stage - me + parts, parts)
        for number in range(parts):

            @pl.when(target == number)
            def _():
                outs[number][0, 0] = real
                if number == LATE:
                    outs[parts][0, 0] = imag
                else:
                    outs[number][0, 1] = imag


def run_chain(me, quarter, kept, start, coupling, arrived, quarters):
    parts = len(arrived) + 1
    orb = start.shape[-1]
    outs = [jax.ShapeDtypeStruct((1, 2, orb, orb), F32)] * parts
    outs[LATE] = jax.ShapeDtypeStruct((1, 1, orb, orb), F32)
    outs.append(outs[LATE])
    return pl.pallas_call(
        lambda *refs: chain_kernel(parts, *refs),
        out_shape=outs,
        in_specs=[SMEM] * 2 + [VMEM] * (3 + len(arrived) + len(quarters)),
        out_specs=[VMEM] * (parts + 1),
        scratch_shapes=[
            pltpu.VMEM((parts, 3, orb, orb), BF16),
            pltpu.VMEM((parts, 3, orb, orb), BF16),
            pltpu.VMEM((parts, 2, orb, orb), F32),
            pltpu.VMEM((2, orb, orb), F32),
            pltpu.VMEM((parts, orb, orb), F32),
        ],
        compiler_params=PARAMS,
        cost_estimate=pl.CostEstimate(
            flops=parts * 48 * orb**3,
            bytes_accessed=parts * 20 * orb * orb,
            transcendentals=0,
        ),
        name="chain",
    )(me, quarter, kept, start, coupling, *arrived, *quarters)


def mix(weights, columns, values, row):
    total = weights[row, columns[0]] * values[0]
    for column, value in zip(columns[1:], values[1:]):
        total = total + weights[row, column] * value
    return total


def early_kernel(count, scalars, weights, *refs):
    slots = refs[: 2 * len(EARLY)]
    green, partial, sems = refs[2 * len(EARLY) :]
    me = scalars[0]
    orb = partial.shape[-1]
    copies = []
    for number, shift in enumerate(EARLY):
        place = lax.rem(me - shift + count, count)
        copies.append(pltpu.make_async_copy(slots[number].at[0], green.at[place], sems.at[number]))
    for copy in copies:
        copy.start()
    columns = list(EARLY) + [count + shift for shift in EARLY]
    rows = 32
    for half in range(2):

        @pl.loop(0, orb // rows)
        def _(step):
            place = pl.ds(pl.multiple_of(step * rows, rows), rows)
            values = [slot[0, half, place, :] for slot in slots]
            for row in range(count):
                partial[half, row, place, :] = mix(weights, columns, values, row)

    for copy in copies:
        copy.wait()


def run_early(me, weights, slots):
    count = weights.shape[0]
    orb = slots[0].shape[-1]
    return pl.pallas_call(
        lambda *refs: early_kernel(count, *refs),
        out_shape=[
            jax.ShapeDtypeStruct((count, 2, orb, orb), F32),
            jax.ShapeDtypeStruct((2, count, orb, orb), F32),
        ],
        in_specs=[SMEM, SMEM] + [VMEM] * len(slots),
        out_specs=[HBM, VMEM],
        scratch_shapes=[pltpu.SemaphoreType.DMA((len(EARLY),))],
        compiler_params=SMALL,
        cost_estimate=pl.CostEstimate(
            flops=0, bytes_accessed=64 * orb * orb, transcendentals=0
        ),
        name="band_early",
    )(me[None], weights, *slots)


def late_kernel(count, me_ref, weights, partial, *refs):
    slots, halos = refs[:2], refs[2:4]
    green, energy, done, sems = refs[5:]
    orb = partial.shape[-1]
    place = lax.rem(me_ref[0] - LATE + count, count)
    copies = []
    for half, slot in enumerate(slots):
        copies.append(pltpu.make_async_copy(slot.at[0, 0], green.at[place, half], sems.at[half]))
        copies[-1].start()
    for row in range(count):
        for half in range(2):

            @pl.loop(0, orb // ROWS)
            def _(step):
                where = pl.ds(pl.multiple_of(step * ROWS, ROWS), ROWS)
                values = [slots[half][0, 0, where, :], halos[half][0, 0, where, :]]
                done[row, half, where, :] = partial[half, row, where, :] + mix(
                    weights, (LATE, count + LATE), values, row
                )

        copy = pltpu.make_async_copy(done.at[row], energy.at[row], sems.at[2 + row])
        copy.start()
        copies.append(copy)
    for copy in copies:
        copy.wait()


def run_late(me, weights, partial, slots, halos, green):
    count = weights.shape[0]
    whole = jax.ShapeDtypeStruct(green.shape, F32)
    return pl.pallas_call(
        lambda *refs: late_kernel(count, *refs),
        out_shape=[whole] * 2,
        in_specs=[SMEM, SMEM] + [VMEM] * 5 + [HBM],
        out_specs=[HBM] * 2,
        input_output_aliases={7: 0},
        scratch_shapes=[pltpu.VMEM(green.shape, F32), pltpu.SemaphoreType.DMA((2 + count,))],
        compiler_params=SMALL,
        name="band_late",
    )(me[None], weights, partial, *slots, *halos, green)


def admit_kernel(value, kept):
    pass


def run_admit(value):
    return pl.pallas_call(
        admit_kernel,
        out_shape=jax.ShapeDtypeStruct(value.shape, F32),
        in_specs=[VMEM],
        out_specs=VMEM,
        input_output_aliases={0: 0},
        compiler_params=SMALL,
        cost_estimate=pl.CostEstimate(flops=1_000_000_000, bytes_accessed=0, transcendentals=0),
        name="admit",
    )(value)


def on_device(inverse_blocks, coupling, boundary, band_offsets, band_weights):
    parts, devices = lax.axis_size("sec"), lax.axis_size("en")
    own_inverse = inverse_blocks[0]
    count = own_inverse.shape[0]
    me, lane = lax.axis_index("sec"), lax.axis_index("en")
    orb = coupling.shape[-1]
    rows = orb // 4
    core = lax.rem(lane, 2)
    quarter = core + 2 * lax.rem(lane // 2 + lane // 16, 2)
    both = ("sec", "en")

    def ring(value, shift):
        pairs = [(source, (source + shift) % parts) for source in range(parts)]
        return lax.ppermute(value, "sec", pairs)

    def halo(value, shift):
        pairs = []
        for sec in range(parts):
            step = 1 if (sec - shift) % parts >= count // 2 else -1
            for en in range(devices):
                if 0 <= en + step < devices:
                    pairs.append((sec * devices + en, sec * devices + en + step))
        return lax.ppermute(value, both, pairs)

    def after(values, *waits):
        return list(lax.optimization_barrier((tuple(values), waits))[0])

    sent = [
        lax.dynamic_slice_in_dim(own_inverse, lax.rem(me + shift, parts), 1, axis=0)
        for shift in range(1, parts)
    ]
    piece = lax.dynamic_slice(coupling, (0, quarter * rows, 0), (1, rows, orb))
    piece = after([piece], *sent)[0]
    gathered = [ring(piece, shift) for shift in range(1, parts)]
    arrived = [ring(value, shift) for shift, value in enumerate(sent, 1)]
    first = jnp.concatenate(gathered, axis=0)
    partners = (0, 1, 2, 17)
    quarters = [first] + [
        lax.ppermute(first, "en", [(source, source ^ partner) for source in range(devices)])
        for partner in partners[1:]
    ]
    kept, start = run_pick(me[None], own_inverse, boundary)

    produced = run_chain(me[None], quarter[None], kept, start, coupling, arrived, quarters)
    early = [produced[0]] + [ring(produced[shift], shift) for shift in EARLY[1:]]
    halos = [halo(early[0], 0)]
    early[1:] = [run_admit(value) for value in early[1:]]
    late = after([produced[LATE], produced[parts]], *early[1:], *halos)
    late = [ring(value, LATE) for value in late]
    halos += [halo(value, shift) for shift, value in zip(EARLY[1:], early[1:])]
    late_halos = [halo(value, LATE) for value in late]

    local = lax.rem(me - jnp.arange(parts, dtype=jnp.int32) + parts, parts)
    beyond = jnp.where(local >= count // 2, local - count, local + count)
    place = jnp.concatenate([local, beyond])
    away = place[None, :] - jnp.arange(count, dtype=jnp.int32)[:, None]
    hits = (band_offsets[:, None, None] == away[None]).astype(F32)
    weights = jnp.sum(band_weights[0][:, None, None] * hits, axis=0)
    green, partial = run_early(me, weights, early + halos)
    green, energy = run_late(me, weights, partial, late, late_halos, green)
    return green[None], energy[None]


def solution(mesh):
    return jax.shard_map(
        on_device,
        mesh=mesh,
        in_specs=(
            P("sec", "en", None, None, None),
            P("sec", None, None),
            P("en", None, None, None),
            P(),
            P("sec", None),
        ),
        out_specs=(P("sec", "en", None, None, None), P("sec", "en", None, None, None)),
        check_vma=False,
    )
```

```python
import jax
import jax.numpy as jnp
from jax import lax
from jax.experimental import pallas as pl
from jax.experimental.pallas import tpu as pltpu
from jax.sharding import PartitionSpec as P

F32 = jnp.float32
BF16 = jnp.bfloat16
NN = (((1,), (0,)), ((), ()))
NT = (((1,), (1,)), ((), ()))
VMEM = pl.BlockSpec(memory_space=pltpu.VMEM)
SMEM = pl.BlockSpec(memory_space=pltpu.SMEM)
HBM = pl.BlockSpec(memory_space=pltpu.HBM)
PARAMS = pltpu.CompilerParams(vmem_limit_bytes=36 * 1024 * 1024)
EARLY = (0, 1, 3)
ROWS = 32
LATE = 2
FIRST = 3
SMALL = pltpu.CompilerParams(vmem_limit_bytes=8 * 1024 * 1024)
def split(value):
    high = value.astype(BF16)
    return high, (value - high.astype(F32)).astype(BF16)


def dot3(left, right, dims):
    def one(a, b):
        return lax.dot_general(a, b, dims, preferred_element_type=F32)

    return one(left[0], right[0]) + (one(left[0], right[1]) + one(left[1], right[0]))


def triple(real, imag):
    return split(real), split(imag), split(real + imag)


def gauss(left, right, dims):
    first, second, third = (dot3(a, b, dims) for a, b in zip(left, right))
    return first - second, third - first - second


def store_transfer(inverse, coupling, high, low, stage):
    orb = coupling.shape[-1]
    both = dot3(split(inverse.reshape(2 * orb, orb)), split(coupling), NN)
    for number, (upper, lower) in enumerate(triple(both[:orb], both[orb:])):
        high[stage, number] = upper
        low[stage, number] = lower


def pick_kernel(me, inverse_all, boundary_all, kept, start, sems):
    copies = [
        pltpu.make_async_copy(inverse_all.at[me[0]], kept, sems.at[0]),
        pltpu.make_async_copy(boundary_all.at[me[0]], start, sems.at[1]),
    ]
    for copy in copies:
        copy.start()
    for copy in copies:
        copy.wait()


def run_pick(me, inverse_blocks, boundary):
    block = jax.ShapeDtypeStruct(inverse_blocks.shape[1:], F32)
    return pl.pallas_call(
        pick_kernel,
        out_shape=[block] * 2,
        in_specs=[SMEM] + [HBM] * 2,
        out_specs=[VMEM] * 2,
        scratch_shapes=[pltpu.SemaphoreType.DMA((2,))],
        compiler_params=SMALL,
        name="pick",
    )(me, inverse_blocks, boundary)


def prepare_kernel(parts, me_ref, quarter_ref, kept, own_coupling, arrived, *refs):
    quarters = refs[:parts]
    high, low, inverse, coupling = refs[parts:]
    me = me_ref[0]
    rows = coupling.shape[-1] // len(quarters)
    coupling[0] = own_coupling[0]
    for number, source in enumerate(quarters):
        quarter = lax.bitwise_xor(quarter_ref[0], number)
        place = pl.ds(pl.multiple_of(quarter * rows, rows), rows)
        for shift in range(1, parts):
            coupling[shift, place, :] = source[shift - 1]
    for shift, block in ((0, kept[...]), (FIRST, arrived[0])):
        stage = lax.rem(me - shift + parts, parts)
        inverse[stage] = block
        store_transfer(block, coupling[shift], high, low, stage)


def run_prepare(me, quarter, kept, coupling, arrived, quarters):
    parts, orb = len(quarters), kept.shape[-1]
    return pl.pallas_call(
        lambda *refs: prepare_kernel(parts, *refs),
        out_shape=[
            jax.ShapeDtypeStruct((parts, 3, orb, orb), BF16),
            jax.ShapeDtypeStruct((parts, 3, orb, orb), BF16),
            jax.ShapeDtypeStruct((parts, 2, orb, orb), F32),
            jax.ShapeDtypeStruct((parts, orb, orb), F32),
        ],
        in_specs=[SMEM] * 2 + [VMEM] * (3 + parts),
        out_specs=[VMEM] * 4,
        compiler_params=PARAMS,
        name="prepare",
    )(me, quarter, kept, coupling, arrived, *quarters)


def chain_kernel(parts, me_ref, start, coupling, first, second, *refs):
    high, low, inverse = refs[3:6]
    outs, previous = refs[6:-1], refs[-1]
    me = me_ref[0]
    for shift, block in zip([shift for shift in range(1, parts) if shift != FIRST], (first, second)):
        stage = lax.rem(me - shift + parts, parts)
        inverse[stage] = block[0]
        store_transfer(block[0], coupling[shift], high, low, stage)
    previous[...] = start[...]
    for stage in range(parts):
        transfer = [(high[stage, number], low[stage, number]) for number in range(3)]
        half = gauss(transfer, triple(previous[0], previous[1]), NN)
        real, imag = gauss(triple(*half), transfer, NT)
        real = real + inverse[stage, 0]
        imag = imag + inverse[stage, 1]
        if stage < parts - 1:
            previous[0] = real
            previous[1] = imag
        target = lax.rem(stage - me + parts, parts)
        for number in range(parts):

            @pl.when(target == number)
            def _():
                outs[number][0, 0] = real
                if number == LATE:
                    outs[parts][0, 0] = imag
                else:
                    outs[number][0, 1] = imag


def run_chain(me, start, prepared, arrived):
    high, low, inverse, coupling = prepared
    parts, orb = high.shape[0], high.shape[-1]
    outs = [jax.ShapeDtypeStruct(value.shape, value.dtype) for value in (high, low, inverse)]
    outs += [jax.ShapeDtypeStruct((1, 2, orb, orb), F32)] * parts
    outs[3 + LATE] = jax.ShapeDtypeStruct((1, 1, orb, orb), F32)
    outs.append(outs[3 + LATE])
    return pl.pallas_call(
        lambda *refs: chain_kernel(parts, *refs),
        out_shape=outs,
        in_specs=[SMEM] + [VMEM] * 7,
        out_specs=[VMEM] * len(outs),
        input_output_aliases={5: 0, 6: 1, 7: 2},
        scratch_shapes=[pltpu.VMEM((2, orb, orb), F32)],
        compiler_params=PARAMS,
        cost_estimate=pl.CostEstimate(
            flops=parts * 48 * orb**3,
            bytes_accessed=parts * 20 * orb * orb,
            transcendentals=0,
        ),
        name="chain",
    )(me, start, coupling, *arrived, high, low, inverse)[3:]


def mix(weights, columns, values, row):
    total = weights[row, columns[0]] * values[0]
    for column, value in zip(columns[1:], values[1:]):
        total = total + weights[row, column] * value
    return total


def early_kernel(count, scalars, weights, *refs):
    slots = refs[: 2 * len(EARLY)]
    green, partial, sems = refs[2 * len(EARLY) :]
    me = scalars[0]
    orb = partial.shape[-1]
    copies = []
    for number, shift in enumerate(EARLY):
        place = lax.rem(me - shift + count, count)
        copies.append(pltpu.make_async_copy(slots[number].at[0], green.at[place], sems.at[number]))
    for copy in copies:
        copy.start()
    columns = list(EARLY) + [count + shift for shift in EARLY]
    rows = 32
    for half in range(2):

        @pl.loop(0, orb // rows)
        def _(step):
            place = pl.ds(pl.multiple_of(step * rows, rows), rows)
            values = [slot[0, half, place, :] for slot in slots]
            for row in range(count):
                partial[half, row, place, :] = mix(weights, columns, values, row)

    for copy in copies:
        copy.wait()


def run_early(me, weights, slots):
    count = weights.shape[0]
    orb = slots[0].shape[-1]
    return pl.pallas_call(
        lambda *refs: early_kernel(count, *refs),
        out_shape=[
            jax.ShapeDtypeStruct((count, 2, orb, orb), F32),
            jax.ShapeDtypeStruct((2, count, orb, orb), F32),
        ],
        in_specs=[SMEM, SMEM] + [VMEM] * len(slots),
        out_specs=[HBM, VMEM],
        scratch_shapes=[pltpu.SemaphoreType.DMA((len(EARLY),))],
        compiler_params=SMALL,
        cost_estimate=pl.CostEstimate(
            flops=0, bytes_accessed=64 * orb * orb, transcendentals=0
        ),
        name="band_early",
    )(me[None], weights, *slots)


def late_kernel(count, me_ref, weights, partial, *refs):
    slots, halos = refs[:2], refs[2:4]
    green, energy, done, sems = refs[5:]
    orb = partial.shape[-1]
    place = lax.rem(me_ref[0] - LATE + count, count)
    copies = []
    for half, slot in enumerate(slots):
        copies.append(pltpu.make_async_copy(slot.at[0, 0], green.at[place, half], sems.at[half]))
        copies[-1].start()
    for row in range(count):
        for half in range(2):

            @pl.loop(0, orb // ROWS)
            def _(step):
                where = pl.ds(pl.multiple_of(step * ROWS, ROWS), ROWS)
                values = [slots[half][0, 0, where, :], halos[half][0, 0, where, :]]
                done[row, half, where, :] = partial[half, row, where, :] + mix(
                    weights, (LATE, count + LATE), values, row
                )

        copy = pltpu.make_async_copy(done.at[row], energy.at[row], sems.at[2 + row])
        copy.start()
        copies.append(copy)
    for copy in copies:
        copy.wait()


def run_late(me, weights, partial, slots, halos, green):
    count = weights.shape[0]
    whole = jax.ShapeDtypeStruct(green.shape, F32)
    return pl.pallas_call(
        lambda *refs: late_kernel(count, *refs),
        out_shape=[whole] * 2,
        in_specs=[SMEM, SMEM] + [VMEM] * 5 + [HBM],
        out_specs=[HBM] * 2,
        input_output_aliases={7: 0},
        scratch_shapes=[pltpu.VMEM(green.shape, F32), pltpu.SemaphoreType.DMA((2 + count,))],
        compiler_params=SMALL,
        name="band_late",
    )(me[None], weights, partial, *slots, *halos, green)


def admit_kernel(value, kept):
    pass


def run_admit(value):
    return pl.pallas_call(
        admit_kernel,
        out_shape=jax.ShapeDtypeStruct(value.shape, F32),
        in_specs=[VMEM],
        out_specs=VMEM,
        input_output_aliases={0: 0},
        compiler_params=SMALL,
        cost_estimate=pl.CostEstimate(flops=1_000_000_000, bytes_accessed=0, transcendentals=0),
        name="admit",
    )(value)


def on_device(inverse_blocks, coupling, boundary, band_offsets, band_weights):
    parts, devices = lax.axis_size("sec"), lax.axis_size("en")
    own_inverse = inverse_blocks[0]
    count = own_inverse.shape[0]
    me, lane = lax.axis_index("sec"), lax.axis_index("en")
    orb = coupling.shape[-1]
    rows = orb // 4
    core = lax.rem(lane, 2)
    quarter = core + 2 * lax.rem(lane // 2 + lane // 16, 2)
    both = ("sec", "en")

    def ring(value, shift):
        pairs = [(source, (source + shift) % parts) for source in range(parts)]
        return lax.ppermute(value, "sec", pairs)

    def halo(value, shift):
        pairs = []
        for sec in range(parts):
            step = 1 if (sec - shift) % parts >= count // 2 else -1
            for en in range(devices):
                if 0 <= en + step < devices:
                    pairs.append((sec * devices + en, sec * devices + en + step))
        return lax.ppermute(value, both, pairs)

    def after(values, *waits):
        return list(lax.optimization_barrier((tuple(values), waits))[0])

    sent = [
        lax.dynamic_slice_in_dim(own_inverse, lax.rem(me + shift, parts), 1, axis=0)
        for shift in range(1, parts)
    ]
    piece = lax.dynamic_slice(coupling, (0, quarter * rows, 0), (1, rows, orb))
    piece = after([piece], *sent)[0]
    gathered = [ring(piece, shift) for shift in range(1, parts)]
    arrived = [ring(value, shift) for shift, value in enumerate(sent, 1)]
    first = jnp.concatenate(gathered, axis=0)
    partners = (0, 1, 2, 17)
    quarters = [first] + [
        lax.ppermute(first, "en", [(source, source ^ partner) for source in range(devices)])
        for partner in partners[1:]
    ]
    kept, start = run_pick(me[None], own_inverse, boundary)

    prepared = run_prepare(
        me[None], quarter[None], kept, coupling, arrived.pop(FIRST - 1), quarters
    )
    produced = run_chain(me[None], start, prepared, arrived)
    early = [produced[0]] + [ring(produced[shift], shift) for shift in EARLY[1:]]
    halos = [halo(early[0], 0)]
    early[1:] = [run_admit(value) for value in early[1:]]
    late = after([produced[LATE], produced[parts]], *early[1:], *halos)
    late = [ring(value, LATE) for value in late]
    halos += [halo(value, shift) for shift, value in zip(EARLY[1:], early[1:])]
    late_halos = [halo(value, LATE) for value in late]

    local = lax.rem(me - jnp.arange(parts, dtype=jnp.int32) + parts, parts)
    beyond = jnp.where(local >= count // 2, local - count, local + count)
    place = jnp.concatenate([local, beyond])
    away = place[None, :] - jnp.arange(count, dtype=jnp.int32)[:, None]
    hits = (band_offsets[:, None, None] == away[None]).astype(F32)
    weights = jnp.sum(band_weights[0][:, None, None] * hits, axis=0)
    green, partial = run_early(me, weights, early + halos)
    green, energy = run_late(me, weights, partial, late, late_halos, green)
    return green[None], energy[None]


def solution(mesh):
    return jax.shard_map(
        on_device,
        mesh=mesh,
        in_specs=(
            P("sec", "en", None, None, None),
            P("sec", None, None),
            P("en", None, None, None),
            P(),
            P("sec", None),
        ),
        out_specs=(P("sec", "en", None, None, None), P("sec", "en", None, None, None)),
        check_vma=False,
    )
```

```python
import jax
import jax.numpy as jnp
from jax import lax
from jax.experimental import pallas as pl
from jax.experimental.pallas import tpu as pltpu
from jax.sharding import PartitionSpec as P

F32 = jnp.float32
BF16 = jnp.bfloat16
NN = (((1,), (0,)), ((), ()))
NT = (((1,), (1,)), ((), ()))
VMEM = pl.BlockSpec(memory_space=pltpu.VMEM)
SMEM = pl.BlockSpec(memory_space=pltpu.SMEM)
HBM = pl.BlockSpec(memory_space=pltpu.HBM)
PARAMS = pltpu.CompilerParams(vmem_limit_bytes=36 * 1024 * 1024)
EARLY = (0, 1, 3)
ROWS = 32
LATE = 2
FIRST = 3
SMALL = pltpu.CompilerParams(vmem_limit_bytes=8 * 1024 * 1024)
def split(value):
    high = value.astype(BF16)
    return high, (value - high.astype(F32)).astype(BF16)


def dot3(left, right, dims):
    def one(a, b):
        return lax.dot_general(a, b, dims, preferred_element_type=F32)

    return one(left[0], right[0]) + (one(left[0], right[1]) + one(left[1], right[0]))


def triple(real, imag):
    return split(real), split(imag), split(real + imag)


def gauss(left, right, dims):
    first, second, third = (dot3(a, b, dims) for a, b in zip(left, right))
    return first - second, third - first - second


def store_transfer(inverse, coupling, high, low, stage):
    orb = coupling.shape[-1]
    both = dot3(split(inverse.reshape(2 * orb, orb)), split(coupling), NN)
    for number, (upper, lower) in enumerate(triple(both[:orb], both[orb:])):
        high[stage, number] = upper
        low[stage, number] = lower


def pick_kernel(me, inverse_all, boundary_all, kept, start, sems):
    copies = [
        pltpu.make_async_copy(inverse_all.at[me[0]], kept, sems.at[0]),
        pltpu.make_async_copy(boundary_all.at[me[0]], start, sems.at[1]),
    ]
    for copy in copies:
        copy.start()
    for copy in copies:
        copy.wait()


def run_pick(me, inverse_blocks, boundary):
    block = jax.ShapeDtypeStruct(inverse_blocks.shape[1:], F32)
    return pl.pallas_call(
        pick_kernel,
        out_shape=[block] * 2,
        in_specs=[SMEM] + [HBM] * 2,
        out_specs=[VMEM] * 2,
        scratch_shapes=[pltpu.SemaphoreType.DMA((2,))],
        compiler_params=SMALL,
        name="pick",
    )(me, inverse_blocks, boundary)


def prepare_kernel(parts, me_ref, quarter_ref, kept, own_coupling, arrived, *refs):
    quarters = refs[:parts]
    high, low, inverse, coupling = refs[parts:]
    me = me_ref[0]
    rows = coupling.shape[-1] // len(quarters)
    coupling[0] = own_coupling[0]
    for number, source in enumerate(quarters):
        quarter = lax.bitwise_xor(quarter_ref[0], number)
        place = pl.ds(pl.multiple_of(quarter * rows, rows), rows)
        for shift in range(1, parts):
            coupling[shift, place, :] = source[shift - 1]
    for shift, block in ((0, kept[...]), (FIRST, arrived[0])):
        stage = lax.rem(me - shift + parts, parts)
        inverse[stage] = block
        store_transfer(block, coupling[shift], high, low, stage)


def run_prepare(me, quarter, kept, coupling, arrived, quarters):
    parts, orb = len(quarters), kept.shape[-1]
    return pl.pallas_call(
        lambda *refs: prepare_kernel(parts, *refs),
        out_shape=[
            jax.ShapeDtypeStruct((parts, 3, orb, orb), BF16),
            jax.ShapeDtypeStruct((parts, 3, orb, orb), BF16),
            jax.ShapeDtypeStruct((parts, 2, orb, orb), F32),
            jax.ShapeDtypeStruct((parts, orb, orb), F32),
        ],
        in_specs=[SMEM] * 2 + [VMEM] * (3 + parts),
        out_specs=[VMEM] * 4,
        compiler_params=PARAMS,
        name="prepare",
    )(me, quarter, kept, coupling, arrived, *quarters)


def chain_kernel(parts, me_ref, start, coupling, first, second, *refs):
    high, low, inverse = refs[3:6]
    outs, previous = refs[6:-1], refs[-1]
    me = me_ref[0]
    for shift, block in zip([shift for shift in range(1, parts) if shift != FIRST], (first, second)):
        stage = lax.rem(me - shift + parts, parts)
        inverse[stage] = block[0]
        store_transfer(block[0], coupling[shift], high, low, stage)
    previous[...] = start[...]
    for stage in range(parts):
        transfer = [(high[stage, number], low[stage, number]) for number in range(3)]
        half = gauss(transfer, triple(previous[0], previous[1]), NN)
        real, imag = gauss(triple(*half), transfer, NT)
        real = real + inverse[stage, 0]
        imag = imag + inverse[stage, 1]
        if stage < parts - 1:
            previous[0] = real
            previous[1] = imag
        target = lax.rem(stage - me + parts, parts)
        for number in range(parts):

            @pl.when(target == number)
            def _():
                outs[number][0, 0] = real
                if number == LATE:
                    outs[parts][0, 0] = imag
                else:
                    outs[number][0, 1] = imag


def run_chain(me, start, prepared, arrived):
    high, low, inverse, coupling = prepared
    parts, orb = high.shape[0], high.shape[-1]
    outs = [jax.ShapeDtypeStruct(value.shape, value.dtype) for value in (high, low, inverse)]
    outs += [jax.ShapeDtypeStruct((1, 2, orb, orb), F32)] * parts
    outs[3 + LATE] = jax.ShapeDtypeStruct((1, 1, orb, orb), F32)
    outs.append(outs[3 + LATE])
    return pl.pallas_call(
        lambda *refs: chain_kernel(parts, *refs),
        out_shape=outs,
        in_specs=[SMEM] + [VMEM] * 7,
        out_specs=[VMEM] * len(outs),
        input_output_aliases={5: 0, 6: 1, 7: 2},
        scratch_shapes=[pltpu.VMEM((2, orb, orb), F32)],
        compiler_params=PARAMS,
        cost_estimate=pl.CostEstimate(
            flops=parts * 48 * orb**3,
            bytes_accessed=parts * 20 * orb * orb,
            transcendentals=0,
        ),
        name="chain",
    )(me, start, coupling, *arrived, high, low, inverse)[3:]


def mix(weights, columns, values, row):
    total = weights[row, columns[0]] * values[0]
    for column, value in zip(columns[1:], values[1:]):
        total = total + weights[row, column] * value
    return total


def touched(me, count):
    return jnp.where(lax.rem(me - LATE + count, count) >= count // 2, 0, count // 2)


def early_kernel(count, me_ref, weights, *refs):
    wide = len(EARLY)
    slots, halos, late = refs[:wide], refs[wide : 2 * wide], refs[2 * wide : 2 * wide + 2]
    green, energy, rest, done, sems = refs[2 * wide + 2 :]
    me = me_ref[0]
    pair = count // 2
    orb = rest.shape[-1]
    copies = []
    for number, shift in enumerate(EARLY):
        place = lax.rem(me - shift + count, count)
        copies.append(
            pltpu.make_async_copy(slots[number].at[0], green.at[place], sems.at[pair + number])
        )
    place = lax.rem(me - LATE + count, count)
    for half in range(2):
        copies.append(
            pltpu.make_async_copy(
                late[half].at[0, 0], green.at[place, half], sems.at[pair + wide + half]
            )
        )
    for copy in copies:
        copy.start()
    base = touched(me, count)
    columns = list(EARLY) + [count + shift for shift in EARLY] + [LATE]
    for target, first in ((done, pair - base), (rest, base)):
        for half in range(2):

            @pl.loop(0, orb // ROWS)
            def _(step):
                where = pl.ds(pl.multiple_of(step * ROWS, ROWS), ROWS)
                values = [ref[0, half, where, :] for ref in slots + halos]
                values.append(late[half][0, 0, where, :])
                for number in range(pair):
                    target[number, half, where, :] = mix(weights, columns, values, first + number)

        if target is done:
            for number in range(pair):
                copy = pltpu.make_async_copy(
                    done.at[number], energy.at[first + number], sems.at[number]
                )
                copy.start()
                copies.append(copy)
    for copy in copies:
        copy.wait()


def run_early(me, weights, slots, late):
    count = weights.shape[0]
    orb = slots[0].shape[-1]
    whole = jax.ShapeDtypeStruct((count, 2, orb, orb), F32)
    pair = (count // 2, 2, orb, orb)
    return pl.pallas_call(
        lambda *refs: early_kernel(count, *refs),
        out_shape=[whole, whole, jax.ShapeDtypeStruct(pair, F32)],
        in_specs=[SMEM, SMEM] + [VMEM] * (len(slots) + 2),
        out_specs=[HBM, HBM, VMEM],
        scratch_shapes=[
            pltpu.VMEM(pair, F32),
            pltpu.SemaphoreType.DMA((count // 2 + len(EARLY) + 2,)),
        ],
        compiler_params=SMALL,
        cost_estimate=pl.CostEstimate(flops=0, bytes_accessed=64 * orb * orb, transcendentals=0),
        name="band_early",
    )(me[None], weights, *slots, *late)


def late_kernel(count, me_ref, weights, rest, real, imag, _, energy, done, sems):
    orb = rest.shape[-1]
    base = touched(me_ref[0], count)
    copies = []
    for number in range(count // 2):
        row = base + number
        for half, halo in enumerate((real, imag)):

            @pl.loop(0, orb // ROWS)
            def _(step):
                where = pl.ds(pl.multiple_of(step * ROWS, ROWS), ROWS)
                done[number, half, where, :] = (
                    rest[number, half, where, :]
                    + weights[row, count + LATE] * halo[0, 0, where, :]
                )

        copy = pltpu.make_async_copy(done.at[number], energy.at[row], sems.at[number])
        copy.start()
        copies.append(copy)
    for copy in copies:
        copy.wait()


def run_late(me, weights, rest, halos, energy):
    count = weights.shape[0]
    return pl.pallas_call(
        lambda *refs: late_kernel(count, *refs),
        out_shape=jax.ShapeDtypeStruct(energy.shape, F32),
        in_specs=[SMEM, SMEM] + [VMEM] * 3 + [HBM],
        out_specs=HBM,
        input_output_aliases={5: 0},
        scratch_shapes=[
            pltpu.VMEM(rest.shape, F32),
            pltpu.SemaphoreType.DMA((count // 2,)),
        ],
        compiler_params=SMALL,
        name="band_late",
    )(me[None], weights, rest, *halos, energy)


def admit_kernel(value, kept):
    pass


def run_admit(value):
    return pl.pallas_call(
        admit_kernel,
        out_shape=jax.ShapeDtypeStruct(value.shape, F32),
        in_specs=[VMEM],
        out_specs=VMEM,
        input_output_aliases={0: 0},
        compiler_params=SMALL,
        cost_estimate=pl.CostEstimate(flops=1_000_000_000, bytes_accessed=0, transcendentals=0),
        name="admit",
    )(value)


def on_device(inverse_blocks, coupling, boundary, band_offsets, band_weights):
    parts, devices = lax.axis_size("sec"), lax.axis_size("en")
    own_inverse = inverse_blocks[0]
    count = own_inverse.shape[0]
    me, lane = lax.axis_index("sec"), lax.axis_index("en")
    orb = coupling.shape[-1]
    rows = orb // 4
    core = lax.rem(lane, 2)
    quarter = core + 2 * lax.rem(lane // 2 + lane // 16, 2)
    both = ("sec", "en")

    def ring(value, shift):
        pairs = [(source, (source + shift) % parts) for source in range(parts)]
        return lax.ppermute(value, "sec", pairs)

    def halo(value, shift):
        pairs = []
        for sec in range(parts):
            step = 1 if (sec - shift) % parts >= count // 2 else -1
            for en in range(devices):
                if 0 <= en + step < devices:
                    pairs.append((sec * devices + en, sec * devices + en + step))
        return lax.ppermute(value, both, pairs)

    def after(values, *waits):
        return list(lax.optimization_barrier((tuple(values), waits))[0])

    sent = [
        lax.dynamic_slice_in_dim(own_inverse, lax.rem(me + shift, parts), 1, axis=0)
        for shift in range(1, parts)
    ]
    piece = lax.dynamic_slice(coupling, (0, quarter * rows, 0), (1, rows, orb))
    piece = after([piece], *sent)[0]
    gathered = [ring(piece, shift) for shift in range(1, parts)]
    arrived = [ring(value, shift) for shift, value in enumerate(sent, 1)]
    first = jnp.concatenate(gathered, axis=0)
    partners = (0, 1, 2, 17)
    quarters = [first] + [
        lax.ppermute(first, "en", [(source, source ^ partner) for source in range(devices)])
        for partner in partners[1:]
    ]
    kept, start = run_pick(me[None], own_inverse, boundary)

    prepared = run_prepare(
        me[None], quarter[None], kept, coupling, arrived.pop(FIRST - 1), quarters
    )
    produced = run_chain(me[None], start, prepared, arrived)
    early = [produced[0]] + [ring(produced[shift], shift) for shift in EARLY[1:]]
    halos = [halo(early[0], 0)]
    early[1:] = [run_admit(value) for value in early[1:]]
    late = after([produced[LATE], produced[parts]], *early[1:], *halos)
    late = [ring(value, LATE) for value in late]
    halos += [halo(value, shift) for shift, value in zip(EARLY[1:], early[1:])]
    late_halos = [halo(value, LATE) for value in late]

    local = lax.rem(me - jnp.arange(parts, dtype=jnp.int32) + parts, parts)
    beyond = jnp.where(local >= count // 2, local - count, local + count)
    place = jnp.concatenate([local, beyond])
    away = place[None, :] - jnp.arange(count, dtype=jnp.int32)[:, None]
    hits = (band_offsets[:, None, None] == away[None]).astype(F32)
    weights = jnp.sum(band_weights[0][:, None, None] * hits, axis=0)
    green, energy, rest = run_early(me, weights, early + halos, late)
    energy = run_late(me, weights, rest, late_halos, energy)
    return green[None], energy[None]


def solution(mesh):
    return jax.shard_map(
        on_device,
        mesh=mesh,
        in_specs=(
            P("sec", "en", None, None, None),
            P("sec", None, None),
            P("en", None, None, None),
            P(),
            P("sec", None),
        ),
        out_specs=(P("sec", "en", None, None, None), P("sec", "en", None, None, None)),
        check_vma=False,
    )
```
